32 devices in a mesh: row: 16 (over z, y, x), col: 2 (over core).
Axes of the slice: x: 2, y: 2, z: 4, core: 2. Of those that a mesh axis runs over, the one named last changes fastest.
Arguments:
- vectors: float32 [6144, 64], P(('row', 'col')), may hold values from -6 to 6
- stiff_tiles: float32 [16, 2, 32, 192, 192], P('row', 'col'), may hold values from -0.078125 to 0.078125
- tile_coords: int32 [16, 2, 32, 2], P('row', 'col'), may hold values from 0 to 15, as said below
- tile_valid: int32 [16, 2, 32], P('row', 'col'), may hold values from 0 to 1, as said below
Outputs:
- product: float32 [6144, 64], P(('row', 'col'))
The draws below stay inside these ranges and needn't reach their ends.
Inputs may be any that keep to these rules, and one draw needn't show every extreme that they name: `tile_coords`: valid entries of a device's list are distinct and come before all padding; each list holds at most 32 valid entries, and some list holds exactly 32. A stored tile may lie on either side of the diagonal. Padding entries hold in-range coordinates. `tile_valid`: at least one entry of each list is valid.
All inputs are finite; a program needn't handle non-finite values.
Results may differ from the reference program's by a relative error of at most 0.0001.
Values sent between devices are 32-bit elements; how exact they have to be, the bound alone decides.
A program may use at most 128 MiB of HBM per device.

```python
import jax
import jax.numpy as jnp
from jax import lax

TILE = 192
VECS = 64
BLK_DEV = 1
ITERS = 2
LR = 2
LC = 16
MAXT = 32
NB = 32
N = 6144
N_ROW = 16
N_COL = 2


def tile_plan(key):
    row_count = LC // BLK_DEV
    column_count = LR // BLK_DEV
    slot_count = LR * LC
    slot_rows = jnp.arange(slot_count, dtype=jnp.int32) // LC
    slot_cols = jnp.arange(slot_count, dtype=jnp.int32) % LC

    def one_device(device):
        device_key = jax.random.fold_in(jax.random.fold_in(key, 7), device)
        perm_key, count_key = jax.random.split(device_key)
        ranking = jax.random.permutation(perm_key, slot_count).astype(jnp.int32)
        unused, order = lax.top_k(ranking, MAXT)
        power = jax.random.randint(count_key, (), 0, 4, dtype=jnp.int32)
        target = jnp.right_shift(jnp.int32(MAXT), power)
        target = jnp.where(device == 0, jnp.int32(MAXT), target)
        live_count = jnp.maximum(target, jnp.int32(1))
        live = (jnp.arange(MAXT, dtype=jnp.int32) < live_count).astype(jnp.int32)
        places = jnp.stack([slot_rows[order], slot_cols[order]], -1).astype(jnp.int32)
        return (places, live)
    places, live = jax.vmap(one_device)(jnp.arange(row_count * column_count, dtype=jnp.int32))
    return (places.reshape(row_count, column_count, MAXT, 2), live.reshape(row_count, column_count, MAXT))


def draw_tile_coords(key, part):
    return tile_plan(key)[0]


def draw_tile_valid(key, part):
    return tile_plan(key)[1]


def block_scale(key, dims, cuts, low, top_value):
    loudness = 1.0
    for position, shards_of in cuts:
        draws = jax.random.uniform(jax.random.fold_in(jax.random.fold_in(key, 6), position), (shards_of,), jnp.float32, low / len(cuts), top_value / len(cuts))
        loudness = loudness * jnp.repeat(jnp.exp(draws), dims[position] // shards_of).reshape((-1,) + (1,) * (len(dims) - 1 - position))
    return loudness


def noise(key, shape, spread, limit, shards=(), kind=jnp.bfloat16):
    result = spread * jax.random.normal(key, shape, jnp.float32)
    if shards:
        result = result * block_scale(key, shape, shards, -0.22, 0.18)
    return jnp.clip(result, -limit, limit).astype(kind)


def setup_inputs(seed: int = 0) -> dict:
    arg_keys = jax.random.split(jax.random.key(seed), 5)
    vectors = noise(arg_keys[0], (N, VECS), 1.0, 6.0, ((0, 32),), jnp.float32)
    stiff_tiles = noise(arg_keys[1], (N_ROW, N_COL, MAXT, TILE, TILE), (TILE * MAXT) ** -0.5, 0.078125, ((0, 16), (1, 2)), jnp.float32)
    tile_coords = draw_tile_coords(jax.random.fold_in(arg_keys[4], 71), 0)
    tile_valid = draw_tile_valid(jax.random.fold_in(arg_keys[4], 71), 0)
    return dict(vectors=vectors, stiff_tiles=stiff_tiles, tile_coords=tile_coords, tile_valid=tile_valid)


def reference(vectors, stiff_tiles, tile_coords, tile_valid):
    row_ids = jnp.arange(N_ROW, dtype=jnp.int32)[:, None, None]
    col_ids = jnp.arange(N_COL, dtype=jnp.int32)[None, :, None]
    local_rows = tile_coords[..., 0]
    local_cols = tile_coords[..., 1]
    global_row = row_ids * LR + local_rows
    global_col = ((local_cols // BLK_DEV) * N_COL + col_ids) * BLK_DEV + local_cols % BLK_DEV
    live_mask = tile_valid.astype(jnp.float32)
    mirror = live_mask * (global_row != global_col).astype(jnp.float32)
    devices = N_ROW * N_COL
    inputs = (stiff_tiles.reshape(devices, MAXT, TILE, TILE),
              global_row.reshape(devices, MAXT).astype(jnp.int32),
              global_col.reshape(devices, MAXT).astype(jnp.int32),
              live_mask.reshape(devices, MAXT), mirror.reshape(devices, MAXT))
    current = vectors.reshape(NB, TILE, VECS)
    for repeat in range(ITERS):
        def device_step(accumulated, pieces):
            tile_block, rows_here, cols_here, live_here, mirror_here = pieces
            right_side = current[cols_here]
            left_side = current[rows_here]
            direct = jnp.einsum("tpq,tqk->tpk", tile_block, right_side, precision=lax.Precision.HIGHEST)
            mirrored = jnp.einsum("tqp,tqk->tpk", tile_block, left_side, precision=lax.Precision.HIGHEST)
            accumulated = accumulated.at[rows_here].add(direct * live_here[:, None, None])
            accumulated = accumulated.at[cols_here].add(mirrored * mirror_here[:, None, None])
            return accumulated, None

        start_value = jnp.zeros((NB, TILE, VECS), jnp.float32)
        current, unused = lax.scan(device_step, start_value, inputs)
    return current.reshape(N, VECS)
```

```python
import functools

import jax
import jax.numpy as jnp
from jax import lax
from jax.experimental import pallas as pl
from jax.experimental.pallas import tpu as pltpu
from jax.sharding import PartitionSpec as P

ITERS = 2
MESH = pl.DeviceIdType.MESH
LANES = 128


def split(value):
    high = value.astype(jnp.bfloat16).astype(jnp.float32)
    return high, value - high


def pack_tall(value):
    half = value.shape[0] // 2
    return jnp.concatenate([value[:half], value[half:]], axis=1)


def spread(packed):
    high, low = split(packed)
    width = packed.shape[1] // 2
    left = lax.broadcasted_iota(jnp.int32, packed.shape, 1) < width
    upper = jnp.where(left, high, pltpu.roll(low, width, 1))
    lower = jnp.where(left, pltpu.roll(high, width, 1), low)
    return jnp.concatenate([upper, lower], axis=0)


def fold_tall(total):
    width = total.shape[1] // 2
    half = total.shape[0] // 2
    folded = total + pltpu.roll(total, width, 1)
    left = lax.broadcasted_iota(jnp.int32, (half, total.shape[1]), 1) < width
    return jnp.where(left, folded[:half], folded[half:])


def unpack_wide(packed, vecs, size):
    main = packed[:vecs].T
    tail = packed[vecs:]
    tail = jnp.concatenate([tail[:, : size - LANES], tail[:, size - LANES :]], axis=0).T
    return jnp.concatenate([main, tail], axis=0)


def kernel(
    rows, cols, planes,
    x_ref, slot_ref, tiles_hbm, out_ref,
    tiles, gath, rowg, rpart, rrecv, zsend, zrecv, z2send, z2recv, lhs, total,
    tile_sem, ag_send, ag_recv, cx_send, cx_recv, r1_send, r1_recv, r2_send, r2_recv,
    cy_send, cy_recv,
):
    lines = rows // planes
    size, vecs = x_ref.shape
    row = lax.axis_index("row")
    col = lax.axis_index("col")
    line = row // planes
    plane = row % planes

    load = pltpu.make_async_copy(tiles_hbm, tiles, tile_sem)
    load.start()

    def line_peer(dz):
        return (((line + dz) % lines) * planes + plane, col)

    def plane_peer(d):
        return (line * planes + (plane + d) % planes, col)

    def col_peer(dc):
        return (row, (col + dc) % cols)

    def remote(src, dst, send, recv, where):
        return pltpu.make_async_remote_copy(
            src_ref=src, dst_ref=dst, send_sem=send, recv_sem=recv,
            device_id=where, device_id_type=MESH,
        )

    def ag_line(it, dz):
        return remote(gath.at[it, 0, 0], gath.at[it, dz, 0],
                      ag_send.at[it, dz, 0], ag_recv.at[it, dz, 0], line_peer(dz))

    def ag_plane(it, dz, d):
        return remote(gath.at[it, dz, 0], gath.at[it, dz, d],
                      ag_send.at[it, dz, d], ag_recv.at[it, dz, d], plane_peer(d))

    def col_x(it, dc):
        return remote(gath.at[it, 0, 0], rowg.at[it, dc],
                      cx_send.at[it, dc], cx_recv.at[it, dc], col_peer(dc))

    def rs_plane(it, dz, d):
        return remote(zsend.at[it, dz, d], zrecv.at[it, dz, d],
                      r1_send.at[it, dz, d], r1_recv.at[it, dz, d], plane_peer(d))

    def rs_line(it, dz):
        return remote(z2send.at[it, dz], z2recv.at[it, dz],
                      r2_send.at[it, dz], r2_recv.at[it, dz], line_peer(dz))

    def col_y(it, dc):
        return remote(rpart.at[it, dc], rrecv.at[it, dc],
                      cy_send.at[it, dc], cy_recv.at[it, dc], col_peer(dc))

    barrier = pltpu.get_barrier_semaphore()
    for dz in range(1, lines):
        pl.semaphore_signal(barrier, inc=1, device_id=line_peer(dz), device_id_type=MESH)
    for d in range(1, planes):
        pl.semaphore_signal(barrier, inc=1, device_id=plane_peer(d), device_id_type=MESH)
    for dc in range(1, cols):
        pl.semaphore_signal(barrier, inc=1, device_id=col_peer(dc), device_id_type=MESH)
    first = pack_tall(x_ref[...])
    gath[0, 0, 0] = first
    pl.semaphore_wait(barrier, (lines - 1) + (planes - 1) + (cols - 1))

    def tile_parts(a, b, keep):
        slot = slot_ref[a * rows + b]
        scale = jnp.where(slot >= 0, 1.0, 0.0).astype(jnp.float32) * keep
        block = tiles[jnp.maximum(slot, 0)] * scale
        high = block.astype(jnp.bfloat16)
        low = (block - high.astype(jnp.float32)).astype(jnp.bfloat16)
        return high, low

    def mirrored(it, dz, d):
        b = ((line + dz) % lines) * planes + (plane + d) % planes
        acc = jnp.zeros((2 * vecs, size), jnp.float32)
        for dc in range(cols):
            a = (col - dc + cols) % cols
            keep = jnp.where(b == row, 0.0, 1.0).astype(jnp.float32) if dc == 0 else 1.0
            high, low = tile_parts(a, b, keep)
            left = lhs[dc]
            acc = acc + jnp.dot(left, high, preferred_element_type=jnp.float32)
            acc = acc + jnp.dot(left, low, preferred_element_type=jnp.float32)
        wide = acc[:vecs] + acc[vecs:]
        tail = wide[:, LANES:]
        zsend[it, dz, d, pl.ds(0, vecs), :] = wide[:, :LANES]
        zsend[it, dz, d, pl.ds(vecs, vecs // 2), :] = jnp.concatenate(
            [tail[: vecs // 2], tail[vecs // 2 :]], axis=1
        )

    def direct(it, dz, d):
        b = ((line - dz + lines) % lines) * planes + (plane - d + planes) % planes
        right = spread(gath[it, dz, d]).astype(jnp.bfloat16)
        for dc in range(cols):
            a = (col + dc) % cols
            high, low = tile_parts(a, b, 1.0)
            total[dc] += jnp.dot(high, right, preferred_element_type=jnp.float32) + jnp.dot(
                low, right, preferred_element_type=jnp.float32
            )

    def product(it):
        for dc in range(1, cols):
            col_x(it, dc).start()
        for dz in range(1, lines):
            ag_line(it, dz).start()
        for d in range(1, planes):
            ag_plane(it, 0, d).start()
        lhs[0] = spread(gath[it, 0, 0]).T.astype(jnp.bfloat16)
        for dc in range(1, cols):
            col_x(it, dc).wait_recv()
            lhs[dc] = spread(rowg[it, dc]).T.astype(jnp.bfloat16)
        total[...] = jnp.zeros_like(total)

        def group(dz, carry):
            @pl.when(dz > 0)
            def _():
                ag_line(it, dz).wait_recv()
                for d in range(1, planes):
                    ag_plane(it, dz, d).start()

            def one(d, inner):
                mirrored(it, dz, d)
                rs_plane(it, dz, d).start()
                return inner

            return lax.fori_loop(1, planes, one, carry)

        if True:
            group_first = group
            lax.fori_loop(0, lines, group_first, 0)

        def own(dz, carry):
            mirrored(it, dz, 0)
            direct(it, dz, 0)
            return carry

        lax.fori_loop(0, lines, own, 0)

        def reduce(k, carry):
            dz = lines - 1 - k
            block = zsend[it, dz, 0]
            for d in range(1, planes):
                rs_plane(it, dz, d).wait_recv()
                block = block + zrecv[it, dz, d]
            z2send[it, dz] = block

            @pl.when(dz > 0)
            def _():
                rs_line(it, dz).start()

            return carry

        lax.fori_loop(0, lines, reduce, 0)

        def rest(dz, carry):
            def one(d, inner):
                ag_plane(it, dz, d).wait_recv()
                direct(it, dz, d)
                return inner

            return lax.fori_loop(1, planes, one, carry)

        lax.fori_loop(0, lines, rest, 0)

        for dc in range(1, cols):
            rpart[it, dc] = fold_tall(total[dc])
            col_y(it, dc).start()
        mine = fold_tall(total[0])
        wide = z2send[it, 0]
        for dz in range(1, lines):
            rs_line(it, dz).wait_recv()
            wide = wide + z2recv[it, dz]
        tall = unpack_wide(wide, vecs, size)
        for dc in range(1, cols):
            col_y(it, dc).wait_recv()
            mine = mine + rrecv[it, dc]
        return mine, tall

    def step(it, carry):
        mine, tall = product(it)

        @pl.when(it < ITERS - 1)
        def _():
            gath[lax.rem(it + 1, ITERS), 0, 0] = mine + pack_tall(tall)

        @pl.when(it == ITERS - 1)
        def _():
            half = size // 2
            out_ref[pl.ds(0, half), :] = mine[:, :vecs] + tall[:half]
            out_ref[pl.ds(half, half), :] = mine[:, vecs:] + tall[half:]

        return carry

    load.wait()
    lax.fori_loop(0, ITERS, step, 0)

    def drain(it, carry):
        for dc in range(1, cols):
            col_x(it, dc).wait_send()
            col_y(it, dc).wait_send()
        for dz in range(1, lines):
            ag_line(it, dz).wait_send()
            rs_line(it, dz).wait_send()

        def plane_sends(dz, inner):
            for d in range(1, planes):
                ag_plane(it, dz, d).wait_send()
                rs_plane(it, dz, d).wait_send()
            return inner

        return lax.fori_loop(0, lines, plane_sends, carry)

    lax.fori_loop(0, ITERS, drain, 0)


def local(rows, cols, vectors, stiff_tiles, tile_coords, tile_valid):
    size, vecs = vectors.shape
    count = stiff_tiles.shape[2]
    planes = 4 if rows % 4 == 0 else 1
    lines = rows // planes
    place = tile_coords[0, 0, :, 0] * rows + tile_coords[0, 0, :, 1]
    hit = (place[None, :] == jnp.arange(rows * cols, dtype=jnp.int32)[:, None]) & (
        tile_valid[0, 0][None, :] > 0
    )
    slots = jnp.max(jnp.where(hit, jnp.arange(count, dtype=jnp.int32)[None, :], -1), axis=1)
    block = (size * vecs // LANES, LANES)
    f32 = jnp.float32
    dma = pltpu.SemaphoreType.DMA
    grid = (ITERS, lines, planes)
    return pl.pallas_call(
        functools.partial(kernel, rows, cols, planes),
        out_shape=jax.ShapeDtypeStruct((size, vecs), f32),
        in_specs=[
            pl.BlockSpec(memory_space=pltpu.VMEM),
            pl.BlockSpec(memory_space=pltpu.SMEM),
            pl.BlockSpec(memory_space=pl.ANY),
        ],
        out_specs=pl.BlockSpec(memory_space=pltpu.VMEM),
        scratch_shapes=[
            pltpu.VMEM((count, size, size), f32),
            pltpu.VMEM(grid + block, f32),
            pltpu.VMEM((ITERS, cols) + block, f32),
            pltpu.VMEM((ITERS, cols) + block, f32),
            pltpu.VMEM((ITERS, cols) + block, f32),
            pltpu.VMEM(grid + block, f32),
            pltpu.VMEM(grid + block, f32),
            pltpu.VMEM((ITERS, lines) + block, f32),
            pltpu.VMEM((ITERS, lines) + block, f32),
            pltpu.VMEM((cols, 2 * vecs, size), jnp.bfloat16),
            pltpu.VMEM((cols, size, 2 * vecs), f32),
            dma,
            dma(grid), dma(grid),
            dma((ITERS, cols)), dma((ITERS, cols)),
            dma(grid), dma(grid),
            dma((ITERS, lines)), dma((ITERS, lines)),
            dma((ITERS, cols)), dma((ITERS, cols)),
        ],
        compiler_params=pltpu.CompilerParams(
            collective_id=0, has_side_effects=True, vmem_limit_bytes=48 * 1024 * 1024
        ),
    )(vectors, slots, stiff_tiles[0, 0])


def solution(mesh):
    placed = (
        P(("row", "col"), None),
        P("row", "col", None, None, None),
        P("row", "col", None, None),
        P("row", "col", None),
    )
    return jax.shard_map(
        functools.partial(local, mesh.shape["row"], mesh.shape["col"]),
        mesh=mesh, in_specs=placed, out_specs=P(("row", "col"), None), check_vma=False,
    )
```

```python
import functools

import jax
import jax.numpy as jnp
from jax import lax
from jax.experimental import pallas as pl
from jax.experimental.pallas import tpu as pltpu
from jax.sharding import PartitionSpec as P

ITERS = 2
MESH = pl.DeviceIdType.MESH
LANES = 128


def split(value):
    high = value.astype(jnp.bfloat16).astype(jnp.float32)
    return high, value - high


def pack_tall(value):
    half = value.shape[0] // 2
    return jnp.concatenate([value[:half], value[half:]], axis=1)


def spread(packed):
    high, low = split(packed)
    width = packed.shape[1] // 2
    left = lax.broadcasted_iota(jnp.int32, packed.shape, 1) < width
    upper = jnp.where(left, high, pltpu.roll(low, width, 1))
    lower = jnp.where(left, pltpu.roll(high, width, 1), low)
    return jnp.concatenate([upper, lower], axis=0)


def fold_tall(total):
    width = total.shape[1] // 2
    half = total.shape[0] // 2
    folded = total + pltpu.roll(total, width, 1)
    left = lax.broadcasted_iota(jnp.int32, (half, total.shape[1]), 1) < width
    return jnp.where(left, folded[:half], folded[half:])


def unpack_wide(packed, vecs, size):
    main = packed[:vecs].T
    tail = packed[vecs:]
    tail = jnp.concatenate([tail[:, : size - LANES], tail[:, size - LANES :]], axis=0).T
    return jnp.concatenate([main, tail], axis=0)


def kernel(
    rows, cols, planes,
    x_ref, slot_ref, tiles_hbm, out_ref,
    tiles, gath, rowg, rpart, rrecv, zsend, zrecv, z2send, z2recv, lhs, total,
    tile_sem, ag_send, ag_recv, at_send, at_recv, cx_send, cx_recv, r1_send, r1_recv, rt_send, rt_recv, r2_send, r2_recv,
    cy_send, cy_recv,
):
    lines = rows // planes
    vecs, size = x_ref.shape
    half = size // 2
    quarter = half // 2
    row = lax.axis_index("row")
    col = lax.axis_index("col")
    line = row // planes
    plane = row % planes
    up = plane // 2
    side = plane % 2

    load = pltpu.make_async_copy(tiles_hbm, tiles, tile_sem)
    load.start()

    def flipped(d):
        if d == 0:
            return plane
        if d == 1:
            return up * 2 + 1 - side
        if d == 2:
            return (1 - up) * 2 + side
        return (1 - up) * 2 + 1 - side

    def line_peer(dz):
        return (((line + dz) % lines) * planes + plane, col)

    def plane_peer(d):
        return (line * planes + flipped(d), col)

    def col_peer(dc):
        return (row, (col + dc) % cols)

    def remote(src, dst, send, recv, where):
        return pltpu.make_async_remote_copy(
            src_ref=src, dst_ref=dst, send_sem=send, recv_sem=recv,
            device_id=where, device_id_type=MESH,
        )

    def ag_line(it, dz):
        return remote(gath.at[it, 0, 0], gath.at[it, dz, 0],
                      ag_send.at[it, dz, 0], ag_recv.at[it, dz, 0], line_peer(dz))

    def ag_plane(it, dz, d):
        return remote(gath.at[it, dz, 0], gath.at[it, dz, d],
                      ag_send.at[it, dz, d], ag_recv.at[it, dz, d], plane_peer(d))

    def ag_turn(it, dz, h):
        part = pl.ds(h * quarter, quarter)
        return remote(gath.at[it, dz, 1 + h, part], gath.at[it, dz, 3, part],
                      at_send.at[it, dz, h], at_recv.at[it, dz, h], plane_peer(2 - h))

    def col_x(it, dc):
        return remote(gath.at[it, 0, 0], rowg.at[it, dc],
                      cx_send.at[it, dc], cx_recv.at[it, dc], col_peer(dc))

    def rs_turn(it, dz, h):
        part = pl.ds(h * quarter, quarter)
        return remote(zsend.at[it, dz, 3, part], zrecv.at[it, dz, 3, part],
                      rt_send.at[it, dz, h], rt_recv.at[it, dz, h], plane_peer(1 + h))

    def rs_plane(it, dz, d):
        return remote(zsend.at[it, dz, d], zrecv.at[it, dz, d],
                      r1_send.at[it, dz, d], r1_recv.at[it, dz, d], plane_peer(d))

    def rs_line(it, dz):
        return remote(z2send.at[it, dz], z2recv.at[it, dz],
                      r2_send.at[it, dz], r2_recv.at[it, dz], line_peer(dz))

    def col_y(it, dc):
        return remote(rpart.at[it, dc], rrecv.at[it, dc],
                      cy_send.at[it, dc], cy_recv.at[it, dc], col_peer(dc))

    barrier = pltpu.get_barrier_semaphore()
    for dz in range(1, lines):
        pl.semaphore_signal(barrier, inc=1, device_id=line_peer(dz), device_id_type=MESH)
    for d in range(1, 3):
        pl.semaphore_signal(barrier, inc=1, device_id=plane_peer(d), device_id_type=MESH)
    for dc in range(1, cols):
        pl.semaphore_signal(barrier, inc=1, device_id=col_peer(dc), device_id_type=MESH)
    gath[0, 0, 0] = pack_tall(
        jnp.concatenate([x_ref[:, :LANES].T, x_ref[:, LANES:].T], axis=0)
    )
    pl.semaphore_wait(barrier, (lines - 1) + 2 + (cols - 1))

    def tile_parts(a, b, keep):
        slot = slot_ref[a * rows + b]
        scale = jnp.where(slot >= 0, 1.0, 0.0).astype(jnp.float32) * keep
        block = tiles[jnp.maximum(slot, 0)] * scale
        high = block.astype(jnp.bfloat16)
        low = (block - high.astype(jnp.float32)).astype(jnp.bfloat16)
        return high, low

    def mirrored(it, dz, d):
        b = ((line + dz) % lines) * planes + flipped(d)
        acc = jnp.zeros((2 * vecs, size), jnp.float32)
        for dc in range(cols):
            a = (col - dc + cols) % cols
            keep = jnp.where(b == row, 0.0, 1.0).astype(jnp.float32) if dc == 0 else 1.0
            high, low = tile_parts(a, b, keep)
            left = lhs[dc]
            acc = acc + jnp.dot(left, high, preferred_element_type=jnp.float32)
            acc = acc + jnp.dot(left, low, preferred_element_type=jnp.float32)
        wide = acc[:vecs] + acc[vecs:]
        tail = wide[:, LANES:]
        return jnp.concatenate(
            [
                wide[:, :LANES],
                jnp.concatenate([tail[: vecs // 2], tail[vecs // 2 :]], axis=1),
            ],
            axis=0,
        )

    def direct(it, dz, d):
        b = ((line - dz + lines) % lines) * planes + flipped(d)
        right = spread(gath[it, dz, d]).astype(jnp.bfloat16)
        for dc in range(cols):
            a = (col + dc) % cols
            high, low = tile_parts(a, b, 1.0)
            total[dc] += jnp.dot(high, right, preferred_element_type=jnp.float32) + jnp.dot(
                low, right, preferred_element_type=jnp.float32
            )

    def product(it):
        for dz in range(1, lines):
            ag_line(it, dz).start()
        for dc in range(1, cols):
            col_x(it, dc).start()
        for d in range(1, 3):
            ag_plane(it, 0, d).start()
        lhs[0] = spread(gath[it, 0, 0]).T.astype(jnp.bfloat16)
        for dc in range(1, cols):
            col_x(it, dc).wait_recv()
            lhs[dc] = spread(rowg[it, dc]).T.astype(jnp.bfloat16)
        total[...] = jnp.zeros_like(total)

        @pl.when(it == 0)
        def _():
            load.wait()

        def corner(dz, carry):
            zsend[it, dz, 3] = mirrored(it, dz, 3)
            for h in range(2):
                rs_turn(it, dz, h).start()
            return carry

        lax.fori_loop(0, lines, corner, 0)

        def group(dz, carry):
            @pl.when(dz > 0)
            def _():
                ag_line(it, dz).wait_recv()
                for d in range(1, 3):
                    ag_plane(it, dz, d).start()

            one = mirrored(it, dz, 1)
            rs_turn(it, dz, 1).wait_recv()
            zsend[it, dz, 1, pl.ds(0, quarter), :] = one[:quarter]
            zsend[it, dz, 1, pl.ds(quarter, quarter), :] = (
                one[quarter:] + zrecv[it, dz, 3, pl.ds(quarter, quarter), :]
            )
            rs_plane(it, dz, 1).start()
            two = mirrored(it, dz, 2)
            rs_turn(it, dz, 0).wait_recv()
            zsend[it, dz, 2, pl.ds(0, quarter), :] = (
                two[:quarter] + zrecv[it, dz, 3, pl.ds(0, quarter), :]
            )
            zsend[it, dz, 2, pl.ds(quarter, quarter), :] = two[quarter:]
            rs_plane(it, dz, 2).start()
            return carry

        lax.fori_loop(0, lines, group, 0)

        def own(dz, carry):
            for h in range(2):
                ag_plane(it, dz, 1 + h).wait_recv()
                ag_turn(it, dz, h).start()
            zsend[it, dz, 0] = mirrored(it, dz, 0)
            direct(it, dz, 0)
            return carry

        lax.fori_loop(0, lines, own, 0)

        def reduce(k, carry):
            dz = lines - 1 - k
            block = zsend[it, dz, 0]
            for d in range(1, 3):
                rs_plane(it, dz, d).wait_recv()
                block = block + zrecv[it, dz, d]
            z2send[it, dz] = block

            @pl.when(dz > 0)
            def _():
                rs_line(it, dz).start()

            return carry

        lax.fori_loop(0, lines, reduce, 0)

        def sides(dz, carry):
            for d in range(1, 3):
                direct(it, dz, d)
            return carry

        lax.fori_loop(0, lines, sides, 0)

        def last(dz, carry):
            for h in range(2):
                ag_turn(it, dz, h).wait_recv()
            direct(it, dz, 3)
            return carry

        lax.fori_loop(0, lines, last, 0)

        for dc in range(1, cols):
            rpart[it, dc] = fold_tall(total[dc])
            col_y(it, dc).start()
        mine = fold_tall(total[0])
        wide = z2send[it, 0]
        for dz in range(1, lines):
            rs_line(it, dz).wait_recv()
            wide = wide + z2recv[it, dz]
        tall = unpack_wide(wide, vecs, size)
        for dc in range(1, cols):
            col_y(it, dc).wait_recv()
            mine = mine + rrecv[it, dc]
        return mine + pack_tall(tall)

    def step(it, carry):
        result = product(it)

        @pl.when(it < ITERS - 1)
        def _():
            gath[lax.rem(it + 1, ITERS), 0, 0] = result

        @pl.when(it == ITERS - 1)
        def _():
            tall = jnp.concatenate([result[:, :vecs], result[:, vecs:]], axis=0)
            out_ref[:, pl.ds(0, LANES)] = tall[:LANES].T
            out_ref[:, pl.ds(LANES, size - LANES)] = tall[LANES:].T

        return carry

    lax.fori_loop(0, ITERS, step, 0)

    def drain(it, carry):
        for dc in range(1, cols):
            col_x(it, dc).wait_send()
            col_y(it, dc).wait_send()
        for dz in range(1, lines):
            ag_line(it, dz).wait_send()
            rs_line(it, dz).wait_send()

        def plane_sends(dz, inner):
            for d in range(1, 3):
                ag_plane(it, dz, d).wait_send()
                rs_plane(it, dz, d).wait_send()
            for h in range(2):
                ag_turn(it, dz, h).wait_send()
                rs_turn(it, dz, h).wait_send()
            return inner

        return lax.fori_loop(0, lines, plane_sends, carry)

    lax.fori_loop(0, ITERS, drain, 0)


def local(rows, cols, vectors, stiff_tiles, tile_coords, tile_valid):
    size, vecs = vectors.shape
    count = stiff_tiles.shape[2]
    planes = 4
    lines = rows // planes
    place = tile_coords[0, 0, :, 0] * rows + tile_coords[0, 0, :, 1]
    hit = (place[None, :] == jnp.arange(rows * cols, dtype=jnp.int32)[:, None]) & (
        tile_valid[0, 0][None, :] > 0
    )
    slots = jnp.max(jnp.where(hit, jnp.arange(count, dtype=jnp.int32)[None, :], -1), axis=1)
    block = (size * vecs // LANES, LANES)
    f32 = jnp.float32
    dma = pltpu.SemaphoreType.DMA
    grid = (ITERS, lines, planes)
    return pl.pallas_call(
        functools.partial(kernel, rows, cols, planes),
        out_shape=jax.ShapeDtypeStruct((vecs, size), f32),
        in_specs=[
            pl.BlockSpec(memory_space=pltpu.VMEM),
            pl.BlockSpec(memory_space=pltpu.SMEM),
            pl.BlockSpec(memory_space=pl.ANY),
        ],
        out_specs=pl.BlockSpec(memory_space=pltpu.VMEM),
        scratch_shapes=[
            pltpu.VMEM((count, size, size), f32),
            pltpu.VMEM(grid + block, f32),
            pltpu.VMEM((ITERS, cols) + block, f32),
            pltpu.VMEM((ITERS, cols) + block, f32),
            pltpu.VMEM((ITERS, cols) + block, f32),
            pltpu.VMEM(grid + block, f32),
            pltpu.VMEM(grid + block, f32),
            pltpu.VMEM((ITERS, lines) + block, f32),
            pltpu.VMEM((ITERS, lines) + block, f32),
            pltpu.VMEM((cols, 2 * vecs, size), jnp.bfloat16),
            pltpu.VMEM((cols, size, 2 * vecs), f32),
            dma,
            dma(grid), dma(grid),
            dma((ITERS, lines, 2)), dma((ITERS, lines, 2)),
            dma((ITERS, cols)), dma((ITERS, cols)),
            dma(grid), dma(grid),
            dma((ITERS, lines, 2)), dma((ITERS, lines, 2)),
            dma((ITERS, lines)), dma((ITERS, lines)),
            dma((ITERS, cols)), dma((ITERS, cols)),
        ],
        compiler_params=pltpu.CompilerParams(
            collective_id=0, has_side_effects=True, vmem_limit_bytes=48 * 1024 * 1024
        ),
    )(vectors.T, slots, stiff_tiles[0, 0]).T


def solution(mesh):
    placed = (
        P(("row", "col"), None),
        P("row", "col", None, None, None),
        P("row", "col", None, None),
        P("row", "col", None),
    )
    return jax.shard_map(
        functools.partial(local, mesh.shape["row"], mesh.shape["col"]),
        mesh=mesh, in_specs=placed, out_specs=P(("row", "col"), None), check_vma=False,
    )
```

```python
import functools

import jax
import jax.numpy as jnp
from jax import lax
from jax.experimental import pallas as pl
from jax.experimental.pallas import tpu as pltpu
from jax.sharding import PartitionSpec as P

ITERS = 2
MESH = pl.DeviceIdType.MESH
LANES = 128


def split(value):
    high = value.astype(jnp.bfloat16).astype(jnp.float32)
    return high, value - high


def pack_tall(value):
    half = value.shape[0] // 2
    return jnp.concatenate([value[:half], value[half:]], axis=1)


def spread(packed):
    high, low = split(packed)
    width = packed.shape[1] // 2
    left = lax.broadcasted_iota(jnp.int32, packed.shape, 1) < width
    upper = jnp.where(left, high, pltpu.roll(low, width, 1))
    lower = jnp.where(left, pltpu.roll(high, width, 1), low)
    return jnp.concatenate([upper, lower], axis=0)


def fold_tall(total):
    width = total.shape[1] // 2
    half = total.shape[0] // 2
    folded = total + pltpu.roll(total, width, 1)
    left = lax.broadcasted_iota(jnp.int32, (half, total.shape[1]), 1) < width
    return jnp.where(left, folded[:half], folded[half:])


def unpack_wide(packed, vecs, size):
    main = packed[:vecs].T
    tail = packed[vecs:]
    tail = jnp.concatenate([tail[:, : size - LANES], tail[:, size - LANES :]], axis=0).T
    return jnp.concatenate([main, tail], axis=0)


def kernel(
    rows, cols, planes,
    x_hbm, coords_hbm, valid_hbm, tiles_hbm, out_ref,
    x_ref, coords, valid, table, slot_ref,
    tiles, gath, rowg, rpart, rrecv, zsend, zrecv, z2send, z2recv, lhs, total,
    tile_sem, small_sem, ag_send, ag_recv, at_send, at_recv, cx_send, cx_recv, r1_send, r1_recv, rt_send, rt_recv, r2_send, r2_recv,
    cy_send, cy_recv,
):
    lines = rows // planes
    vecs, size = x_hbm.shape
    half = size // 2
    quarter = half // 2
    row = lax.axis_index("row")
    col = lax.axis_index("col")
    line = row // planes
    plane = row % planes
    up = plane // 2
    side = plane % 2

    load = pltpu.make_async_copy(tiles_hbm, tiles, tile_sem)
    small = [
        pltpu.make_async_copy(src, dst, small_sem.at[i])
        for i, (src, dst) in enumerate(((x_hbm, x_ref), (coords_hbm, coords), (valid_hbm, valid)))
    ]
    for copy in small:
        copy.start()
    load.start()

    def flipped(d):
        if d == 0:
            return plane
        if d == 1:
            return up * 2 + 1 - side
        if d == 2:
            return (1 - up) * 2 + side
        return (1 - up) * 2 + 1 - side

    def line_peer(dz):
        return (((line + dz) % lines) * planes + plane, col)

    def plane_peer(d):
        return (line * planes + flipped(d), col)

    def col_peer(dc):
        return (row, (col + dc) % cols)

    def remote(src, dst, send, recv, where):
        return pltpu.make_async_remote_copy(
            src_ref=src, dst_ref=dst, send_sem=send, recv_sem=recv,
            device_id=where, device_id_type=MESH,
        )

    def ag_line(it, dz):
        return remote(gath.at[it, 0, 0], gath.at[it, dz, 0],
                      ag_send.at[it, dz, 0], ag_recv.at[it, dz, 0], line_peer(dz))

    def ag_plane(it, dz, d):
        return remote(gath.at[it, dz, 0], gath.at[it, dz, d],
                      ag_send.at[it, dz, d], ag_recv.at[it, dz, d], plane_peer(d))

    def ag_turn(it, dz, h):
        part = pl.ds(h * quarter, quarter)
        return remote(gath.at[it, dz, 1 + h, part], gath.at[it, dz, 3, part],
                      at_send.at[it, dz, h], at_recv.at[it, dz, h], plane_peer(2 - h))

    def col_x(it, dc):
        return remote(gath.at[it, 0, 0], rowg.at[it, dc],
                      cx_send.at[it, dc], cx_recv.at[it, dc], col_peer(dc))

    def rs_turn(it, dz, h):
        part = pl.ds(h * quarter, quarter)
        return remote(zsend.at[it, dz, 3, part], zrecv.at[it, dz, 3, part],
                      rt_send.at[it, dz, h], rt_recv.at[it, dz, h], plane_peer(1 + h))

    def rs_plane(it, dz, d):
        return remote(zsend.at[it, dz, d], zrecv.at[it, dz, d],
                      r1_send.at[it, dz, d], r1_recv.at[it, dz, d], plane_peer(d))

    def rs_line(it, dz):
        return remote(z2send.at[it, dz], z2recv.at[it, dz],
                      r2_send.at[it, dz], r2_recv.at[it, dz], line_peer(dz))

    def col_y(it, dc):
        return remote(rpart.at[it, dc], rrecv.at[it, dc],
                      cy_send.at[it, dc], cy_recv.at[it, dc], col_peer(dc))

    barrier = pltpu.get_barrier_semaphore()
    for dz in range(1, lines):
        pl.semaphore_signal(barrier, inc=1, device_id=line_peer(dz), device_id_type=MESH)
    for d in range(1, 3):
        pl.semaphore_signal(barrier, inc=1, device_id=plane_peer(d), device_id_type=MESH)
    for dc in range(1, cols):
        pl.semaphore_signal(barrier, inc=1, device_id=col_peer(dc), device_id_type=MESH)
    for copy in small:
        copy.wait()
    place = jnp.where(valid[...] > 0, coords[0:1, :] * rows + coords[1:2, :], -1)
    spots = (rows * cols, place.shape[1])
    hit = lax.broadcasted_iota(jnp.int32, spots, 0) == jnp.broadcast_to(place, spots)
    found = jnp.max(
        jnp.where(hit, lax.broadcasted_iota(jnp.int32, spots, 1), -1), axis=1, keepdims=True
    )
    table[...] = jnp.broadcast_to(found, table.shape)
    fill = pltpu.make_async_copy(table, slot_ref, small_sem.at[3])
    fill.start()
    gath[0, 0, 0] = pack_tall(
        jnp.concatenate([x_ref[:, :LANES].T, x_ref[:, LANES:].T], axis=0)
    )
    pl.semaphore_wait(barrier, (lines - 1) + 2 + (cols - 1))

    def tile_parts(a, b, keep):
        slot = slot_ref[a * rows + b, 0]
        scale = jnp.where(slot >= 0, 1.0, 0.0).astype(jnp.float32) * keep
        block = tiles[jnp.maximum(slot, 0)] * scale
        high = block.astype(jnp.bfloat16)
        low = (block - high.astype(jnp.float32)).astype(jnp.bfloat16)
        return high, low

    def mirrored(it, dz, d):
        b = ((line + dz) % lines) * planes + flipped(d)
        acc = jnp.zeros((2 * vecs, size), jnp.float32)
        for dc in range(cols):
            a = (col - dc + cols) % cols
            keep = jnp.where(b == row, 0.0, 1.0).astype(jnp.float32) if dc == 0 else 1.0
            high, low = tile_parts(a, b, keep)
            left = lhs[dc]
            acc = acc + jnp.dot(left, high, preferred_element_type=jnp.float32)
            acc = acc + jnp.dot(left, low, preferred_element_type=jnp.float32)
        wide = acc[:vecs] + acc[vecs:]
        tail = wide[:, LANES:]
        return jnp.concatenate(
            [
                wide[:, :LANES],
                jnp.concatenate([tail[: vecs // 2], tail[vecs // 2 :]], axis=1),
            ],
            axis=0,
        )

    def direct(it, dz, d):
        b = ((line - dz + lines) % lines) * planes + flipped(d)
        right = spread(gath[it, dz, d]).astype(jnp.bfloat16)
        for dc in range(cols):
            a = (col + dc) % cols
            high, low = tile_parts(a, b, 1.0)
            total[dc] += jnp.dot(high, right, preferred_element_type=jnp.float32) + jnp.dot(
                low, right, preferred_element_type=jnp.float32
            )

    def product(it):
        for dz in range(1, lines):
            ag_line(it, dz).start()
        for dc in range(1, cols):
            col_x(it, dc).start()
        for d in range(1, 3):
            ag_plane(it, 0, d).start()
        lhs[0] = spread(gath[it, 0, 0]).T.astype(jnp.bfloat16)
        total[...] = jnp.zeros_like(total)

        @pl.when(it == 0)
        def _():
            fill.wait()
            load.wait()

        direct(it, 0, 0)
        for dc in range(1, cols):
            col_x(it, dc).wait_recv()
            lhs[dc] = spread(rowg[it, dc]).T.astype(jnp.bfloat16)

        def corner(n, carry):
            dz = (n + 1) % lines
            zsend[it, dz, 3] = mirrored(it, dz, 3)
            for h in range(2):
                rs_turn(it, dz, h).start()
            return carry

        lax.fori_loop(0, lines, corner, 0)

        def group(n, carry):
            dz = (n + 1) % lines
            one = mirrored(it, dz, 1)
            rs_turn(it, dz, 1).wait_recv()
            zsend[it, dz, 1, pl.ds(0, quarter), :] = one[:quarter]
            zsend[it, dz, 1, pl.ds(quarter, quarter), :] = (
                one[quarter:] + zrecv[it, dz, 3, pl.ds(quarter, quarter), :]
            )
            rs_plane(it, dz, 1).start()
            two = mirrored(it, dz, 2)
            rs_turn(it, dz, 0).wait_recv()
            zsend[it, dz, 2, pl.ds(0, quarter), :] = (
                two[:quarter] + zrecv[it, dz, 3, pl.ds(0, quarter), :]
            )
            zsend[it, dz, 2, pl.ds(quarter, quarter), :] = two[quarter:]
            rs_plane(it, dz, 2).start()

            @pl.when(dz > 0)
            def _():
                ag_line(it, dz).wait_recv()
                for d in range(1, 3):
                    ag_plane(it, dz, d).start()

            return carry

        lax.fori_loop(0, lines, group, 0)

        def turn(dz, carry):
            for h in range(2):
                ag_plane(it, dz, 1 + h).wait_recv()
                ag_turn(it, dz, h).start()
            return carry

        def own(n, carry):
            dz = (n + 1) % lines
            mine = mirrored(it, dz, 0)
            for d in range(1, 3):
                rs_plane(it, dz, d).wait_recv()
            z2send[it, dz] = mine + zrecv[it, dz, 1] + zrecv[it, dz, 2]

            @pl.when(dz > 0)
            def _():
                rs_line(it, dz).start()
                direct(it, dz, 0)

            turn(n, 0)
            return carry

        lax.fori_loop(0, lines, own, 0)

        def sides(dz, carry):
            for d in range(1, 3):
                direct(it, dz, d)
            return carry

        lax.fori_loop(0, lines, sides, 0)

        def last(dz, carry):
            for h in range(2):
                ag_turn(it, dz, h).wait_recv()
            direct(it, dz, 3)
            return carry

        lax.fori_loop(0, lines, last, 0)

        for dc in range(1, cols):
            rpart[it, dc] = fold_tall(total[dc])
            col_y(it, dc).start()
        mine = fold_tall(total[0])
        wide = z2send[it, 0]
        for dz in range(1, lines):
            rs_line(it, dz).wait_recv()
            wide = wide + z2recv[it, dz]
        tall = unpack_wide(wide, vecs, size)
        for dc in range(1, cols):
            col_y(it, dc).wait_recv()
            mine = mine + rrecv[it, dc]
        return mine + pack_tall(tall)

    def step(it, carry):
        result = product(it)

        @pl.when(it < ITERS - 1)
        def _():
            gath[lax.rem(it + 1, ITERS), 0, 0] = result

        @pl.when(it == ITERS - 1)
        def _():
            tall = jnp.concatenate([result[:, :vecs], result[:, vecs:]], axis=0)
            out_ref[:, pl.ds(0, LANES)] = tall[:LANES].T
            out_ref[:, pl.ds(LANES, size - LANES)] = tall[LANES:].T

        return carry

    lax.fori_loop(0, ITERS, step, 0)

    def drain(it, carry):
        for dc in range(1, cols):
            col_x(it, dc).wait_send()
            col_y(it, dc).wait_send()
        for dz in range(1, lines):
            ag_line(it, dz).wait_send()
            rs_line(it, dz).wait_send()

        def plane_sends(dz, inner):
            for d in range(1, 3):
                ag_plane(it, dz, d).wait_send()
                rs_plane(it, dz, d).wait_send()
            for h in range(2):
                ag_turn(it, dz, h).wait_send()
                rs_turn(it, dz, h).wait_send()
            return inner

        return lax.fori_loop(0, lines, plane_sends, carry)

    lax.fori_loop(0, ITERS, drain, 0)


def local(rows, cols, vectors, stiff_tiles, tile_coords, tile_valid):
    size, vecs = vectors.shape
    count = stiff_tiles.shape[2]
    planes = 4
    lines = rows // planes
    block = (size * vecs // LANES, LANES)
    f32 = jnp.float32
    dma = pltpu.SemaphoreType.DMA
    grid = (ITERS, lines, planes)
    return pl.pallas_call(
        functools.partial(kernel, rows, cols, planes),
        out_shape=jax.ShapeDtypeStruct((vecs, size), f32),
        in_specs=[
            pl.BlockSpec(memory_space=pl.ANY),
            pl.BlockSpec(memory_space=pl.ANY),
            pl.BlockSpec(memory_space=pl.ANY),
            pl.BlockSpec(memory_space=pl.ANY),
        ],
        out_specs=pl.BlockSpec(memory_space=pltpu.VMEM),
        scratch_shapes=[
            pltpu.VMEM((vecs, size), f32),
            pltpu.VMEM((2, count), jnp.int32),
            pltpu.VMEM((1, count), jnp.int32),
            pltpu.VMEM((rows * cols, LANES), jnp.int32),
            pltpu.SMEM((rows * cols, LANES), jnp.int32),
            pltpu.VMEM((count, size, size), f32),
            pltpu.VMEM(grid + block, f32),
            pltpu.VMEM((ITERS, cols) + block, f32),
            pltpu.VMEM((ITERS, cols) + block, f32),
            pltpu.VMEM((ITERS, cols) + block, f32),
            pltpu.VMEM(grid + block, f32),
            pltpu.VMEM(grid + block, f32),
            pltpu.VMEM((ITERS, lines) + block, f32),
            pltpu.VMEM((ITERS, lines) + block, f32),
            pltpu.VMEM((cols, 2 * vecs, size), jnp.bfloat16),
            pltpu.VMEM((cols, size, 2 * vecs), f32),
            dma,
            dma((4,)),
            dma(grid), dma(grid),
            dma((ITERS, lines, 2)), dma((ITERS, lines, 2)),
            dma((ITERS, cols)), dma((ITERS, cols)),
            dma(grid), dma(grid),
            dma((ITERS, lines, 2)), dma((ITERS, lines, 2)),
            dma((ITERS, lines)), dma((ITERS, lines)),
            dma((ITERS, cols)), dma((ITERS, cols)),
        ],
        compiler_params=pltpu.CompilerParams(
            collective_id=0, has_side_effects=True, vmem_limit_bytes=48 * 1024 * 1024
        ),
    )(vectors.T, tile_coords[0, 0].T, tile_valid[0], stiff_tiles[0, 0]).T


def solution(mesh):
    placed = (
        P(("row", "col"), None),
        P("row", "col", None, None, None),
        P("row", "col", None, None),
        P("row", "col", None),
    )
    return jax.shard_map(
        functools.partial(local, mesh.shape["row"], mesh.shape["col"]),
        mesh=mesh, in_specs=placed, out_specs=P(("row", "col"), None), check_vma=False,
    )
```

```python
import functools

import jax
import jax.numpy as jnp
from jax import lax
from jax.experimental import pallas as pl
from jax.experimental.pallas import tpu as pltpu
from jax.sharding import PartitionSpec as P

ITERS = 2
MESH = pl.DeviceIdType.MESH
LANES = 128
SPLIT, KEEP, READ = range(3)


def split(value):
    high = value.astype(jnp.bfloat16).astype(jnp.float32)
    return high, value - high


def pack_tall(value):
    half = value.shape[0] // 2
    return jnp.concatenate([value[:half], value[half:]], axis=1)


def spread(packed):
    high, low = split(packed)
    width = packed.shape[1] // 2
    left = lax.broadcasted_iota(jnp.int32, packed.shape, 1) < width
    upper = jnp.where(left, high, pltpu.roll(low, width, 1))
    lower = jnp.where(left, pltpu.roll(high, width, 1), low)
    return jnp.concatenate([upper, lower], axis=0)


def fold_tall(total):
    width = total.shape[1] // 2
    half = total.shape[0] // 2
    folded = total + pltpu.roll(total, width, 1)
    left = lax.broadcasted_iota(jnp.int32, (half, total.shape[1]), 1) < width
    return jnp.where(left, folded[:half], folded[half:])


def unpack_wide(packed, vecs, size):
    main = packed[:vecs].T
    tail = packed[vecs:]
    tail = jnp.concatenate([tail[:, : size - LANES], tail[:, size - LANES :]], axis=0).T
    return jnp.concatenate([main, tail], axis=0)


def kernel(
    rows, cols, planes, kept,
    x_hbm, coords_hbm, valid_hbm, tiles_hbm, out_ref,
    x_ref, coords, valid, table, slot_ref,
    tiles, gath, rowg, rpart, rrecv, zsend, zrecv, z2send, z2recv, lhs, total, parts,
    tile_sem, small_sem, ag_send, ag_recv, at_send, at_recv, cx_send, cx_recv, r1_send, r1_recv, rt_send, rt_recv, r2_send, r2_recv,
    cy_send, cy_recv,
):
    lines = rows // planes
    vecs, size = x_hbm.shape
    half = size // 2
    quarter = half // 2
    row = lax.axis_index("row")
    col = lax.axis_index("col")
    line = row // planes
    plane = row % planes
    up = plane // 2
    side = plane % 2

    load = pltpu.make_async_copy(tiles_hbm, tiles, tile_sem)
    small = [
        pltpu.make_async_copy(src, dst, small_sem.at[i])
        for i, (src, dst) in enumerate(((x_hbm, x_ref), (coords_hbm, coords), (valid_hbm, valid)))
    ]
    for copy in small:
        copy.start()
    load.start()

    def flipped(d):
        if d == 0:
            return plane
        if d == 1:
            return up * 2 + 1 - side
        if d == 2:
            return (1 - up) * 2 + side
        return (1 - up) * 2 + 1 - side

    def line_peer(dz):
        return (((line + dz) % lines) * planes + plane, col)

    def plane_peer(d):
        return (line * planes + flipped(d), col)

    def col_peer(dc):
        return (row, (col + dc) % cols)

    def remote(src, dst, send, recv, where):
        return pltpu.make_async_remote_copy(
            src_ref=src, dst_ref=dst, send_sem=send, recv_sem=recv,
            device_id=where, device_id_type=MESH,
        )

    def ag_line(it, dz):
        return remote(gath.at[it, 0, 0], gath.at[it, dz, 0],
                      ag_send.at[it, dz, 0], ag_recv.at[it, dz, 0], line_peer(dz))

    def ag_plane(it, dz, d):
        return remote(gath.at[it, dz, 0], gath.at[it, dz, d],
                      ag_send.at[it, dz, d], ag_recv.at[it, dz, d], plane_peer(d))

    def ag_turn(it, dz, h):
        part = pl.ds(h * quarter, quarter)
        return remote(gath.at[it, dz, 1 + h, part], gath.at[it, dz, 3, part],
                      at_send.at[it, dz, h], at_recv.at[it, dz, h], plane_peer(2 - h))

    def col_x(it, dc):
        return remote(gath.at[it, 0, 0], rowg.at[it, dc],
                      cx_send.at[it, dc], cx_recv.at[it, dc], col_peer(dc))

    def rs_turn(it, dz, h):
        part = pl.ds(h * quarter, quarter)
        return remote(zsend.at[it, dz, 3, part], zrecv.at[it, dz, 3, part],
                      rt_send.at[it, dz, h], rt_recv.at[it, dz, h], plane_peer(1 + h))

    def rs_plane(it, dz, d):
        return remote(zsend.at[it, dz, d], zrecv.at[it, dz, d],
                      r1_send.at[it, dz, d], r1_recv.at[it, dz, d], plane_peer(d))

    def rs_line(it, dz):
        return remote(z2send.at[it, dz], z2recv.at[it, dz],
                      r2_send.at[it, dz], r2_recv.at[it, dz], line_peer(dz))

    def col_y(it, dc):
        return remote(rpart.at[it, dc], rrecv.at[it, dc],
                      cy_send.at[it, dc], cy_recv.at[it, dc], col_peer(dc))

    barrier = pltpu.get_barrier_semaphore()
    for dz in range(1, lines):
        pl.semaphore_signal(barrier, inc=1, device_id=line_peer(dz), device_id_type=MESH)
    for d in range(1, 3):
        pl.semaphore_signal(barrier, inc=1, device_id=plane_peer(d), device_id_type=MESH)
    for dc in range(1, cols):
        pl.semaphore_signal(barrier, inc=1, device_id=col_peer(dc), device_id_type=MESH)
    for copy in small:
        copy.wait()
    place = jnp.where(valid[...] > 0, coords[0:1, :] * rows + coords[1:2, :], -1)
    spots = (rows * cols, place.shape[1])
    hit = lax.broadcasted_iota(jnp.int32, spots, 0) == jnp.broadcast_to(place, spots)
    found = jnp.max(
        jnp.where(hit, lax.broadcasted_iota(jnp.int32, spots, 1), -1), axis=1, keepdims=True
    )
    table[...] = jnp.broadcast_to(found, table.shape)
    fill = pltpu.make_async_copy(table, slot_ref, small_sem.at[3])
    fill.start()
    gath[0, 0, 0] = pack_tall(
        jnp.concatenate([x_ref[:, :LANES].T, x_ref[:, LANES:].T], axis=0)
    )
    pl.semaphore_wait(barrier, (lines - 1) + 2 + (cols - 1))

    def split_tile(spot):
        slot = slot_ref[spot, 0]
        scale = jnp.where(slot >= 0, 1.0, 0.0).astype(jnp.float32)
        block = tiles[jnp.maximum(slot, 0)] * scale
        high = block.astype(jnp.bfloat16)
        low = (block - high.astype(jnp.float32)).astype(jnp.bfloat16)
        return high, low

    def tile_parts(a, b, mode):
        spot = a * rows + b
        if kept and mode == READ:
            return parts[spot, 0], parts[spot, 1]
        high, low = split_tile(spot)
        if kept and mode == KEEP:
            parts[spot, 0] = high
            parts[spot, 1] = low
        return high, low

    def mirrored(it, dz, d):
        b = ((line + dz) % lines) * planes + flipped(d)
        acc = jnp.zeros((2 * vecs, size), jnp.float32)
        for dc in range(cols):
            a = (col - dc + cols) % cols
            high, low = tile_parts(a, b, KEEP if it == 0 else READ)
            left = lhs[dc]
            if dc == 0 and d == 0:
                left = left * jnp.where(b == row, 0.0, 1.0).astype(jnp.bfloat16)
            acc = acc + jnp.dot(left, high, preferred_element_type=jnp.float32)
            acc = acc + jnp.dot(left, low, preferred_element_type=jnp.float32)
        wide = acc[:vecs] + acc[vecs:]
        tail = wide[:, LANES:]
        return jnp.concatenate(
            [
                wide[:, :LANES],
                jnp.concatenate([tail[: vecs // 2], tail[vecs // 2 :]], axis=1),
            ],
            axis=0,
        )

    def direct(it, dz, *flips):
        sums = [None] * cols
        for d in flips:
            b = ((line - dz + lines) % lines) * planes + flipped(d)
            right = spread(gath[it, dz, d]).astype(jnp.bfloat16)
            for dc in range(cols):
                high, low = tile_parts(
                    (col + dc) % cols, b, SPLIT if it == 0 and d == 0 else READ
                )
                term = jnp.dot(high, right, preferred_element_type=jnp.float32) + jnp.dot(
                    low, right, preferred_element_type=jnp.float32
                )
                sums[dc] = term if sums[dc] is None else sums[dc] + term
        for dc in range(cols):
            total[dc] += sums[dc]

    def product(it):
        for dz in range(1, lines):
            ag_line(it, dz).start()
        for dc in range(1, cols):
            col_x(it, dc).start()
        for d in range(1, 3):
            ag_plane(it, 0, d).start()
        lhs[0] = spread(gath[it, 0, 0]).T.astype(jnp.bfloat16)
        total[...] = jnp.zeros_like(total)

        if it == 0:
            fill.wait()
            load.wait()

        direct(it, 0, 0)
        for dc in range(1, cols):
            col_x(it, dc).wait_recv()
            lhs[dc] = spread(rowg[it, dc]).T.astype(jnp.bfloat16)

        def corner(n, carry):
            dz = (n + 1) % lines
            zsend[it, dz, 3] = mirrored(it, dz, 3)
            for h in range(2):
                rs_turn(it, dz, h).start()
            return carry

        lax.fori_loop(0, lines, corner, 0)

        def group(n, carry):
            dz = (n + 1) % lines
            one = mirrored(it, dz, 1)
            rs_turn(it, dz, 1).wait_recv()
            zsend[it, dz, 1, pl.ds(0, quarter), :] = one[:quarter]
            zsend[it, dz, 1, pl.ds(quarter, quarter), :] = (
                one[quarter:] + zrecv[it, dz, 3, pl.ds(quarter, quarter), :]
            )
            rs_plane(it, dz, 1).start()
            two = mirrored(it, dz, 2)
            rs_turn(it, dz, 0).wait_recv()
            zsend[it, dz, 2, pl.ds(0, quarter), :] = (
                two[:quarter] + zrecv[it, dz, 3, pl.ds(0, quarter), :]
            )
            zsend[it, dz, 2, pl.ds(quarter, quarter), :] = two[quarter:]
            rs_plane(it, dz, 2).start()

            @pl.when(dz > 0)
            def _():
                ag_line(it, dz).wait_recv()
                for d in range(1, 3):
                    ag_plane(it, dz, d).start()

            return carry

        lax.fori_loop(0, lines, group, 0)

        def turn(dz, carry):
            for h in range(2):
                ag_plane(it, dz, 1 + h).wait_recv()
                ag_turn(it, dz, h).start()
            return carry

        def own(n, carry):
            dz = (n + 1) % lines
            mine = mirrored(it, dz, 0)
            turn(n, 0)
            direct(it, n, 1, 2)
            for d in range(1, 3):
                rs_plane(it, dz, d).wait_recv()
            z2send[it, dz] = mine + zrecv[it, dz, 1] + zrecv[it, dz, 2]

            @pl.when(dz > 0)
            def _():
                rs_line(it, dz).start()
                direct(it, dz, 0)

            return carry

        lax.fori_loop(0, lines, own, 0)

        def last(dz, carry):
            for h in range(2):
                ag_turn(it, dz, h).wait_recv()
            direct(it, dz, 3)
            return carry

        lax.fori_loop(0, lines, last, 0)

        for dc in range(1, cols):
            rpart[it, dc] = fold_tall(total[dc])
            col_y(it, dc).start()
        mine = fold_tall(total[0])
        wide = z2send[it, 0]
        for dz in range(1, lines):
            rs_line(it, dz).wait_recv()
            wide = wide + z2recv[it, dz]
        tall = unpack_wide(wide, vecs, size)
        for dc in range(1, cols):
            col_y(it, dc).wait_recv()
            mine = mine + rrecv[it, dc]
        return mine + pack_tall(tall)

    for it in range(ITERS):
        result = product(it)
        if it < ITERS - 1:
            gath[it + 1, 0, 0] = result
        else:
            tall = jnp.concatenate([result[:, :vecs], result[:, vecs:]], axis=0)
            out_ref[:, pl.ds(0, LANES)] = tall[:LANES].T
            out_ref[:, pl.ds(LANES, size - LANES)] = tall[LANES:].T

    def drain(it, carry):
        for dc in range(1, cols):
            col_x(it, dc).wait_send()
            col_y(it, dc).wait_send()
        for dz in range(1, lines):
            ag_line(it, dz).wait_send()
            rs_line(it, dz).wait_send()

        def plane_sends(dz, inner):
            for d in range(1, 3):
                ag_plane(it, dz, d).wait_send()
                rs_plane(it, dz, d).wait_send()
            for h in range(2):
                ag_turn(it, dz, h).wait_send()
                rs_turn(it, dz, h).wait_send()
            return inner

        return lax.fori_loop(0, lines, plane_sends, carry)

    lax.fori_loop(0, ITERS, drain, 0)


def local(rows, cols, vectors, stiff_tiles, tile_coords, tile_valid):
    size, vecs = vectors.shape
    count = stiff_tiles.shape[2]
    planes = 4
    lines = rows // planes
    kept = rows * cols * size * size * 4 <= 16 * 1024 * 1024
    block = (size * vecs // LANES, LANES)
    f32 = jnp.float32
    dma = pltpu.SemaphoreType.DMA
    grid = (ITERS, lines, planes)
    return pl.pallas_call(
        functools.partial(kernel, rows, cols, planes, kept),
        out_shape=jax.ShapeDtypeStruct((vecs, size), f32),
        in_specs=[
            pl.BlockSpec(memory_space=pl.ANY),
            pl.BlockSpec(memory_space=pl.ANY),
            pl.BlockSpec(memory_space=pl.ANY),
            pl.BlockSpec(memory_space=pl.ANY),
        ],
        out_specs=pl.BlockSpec(memory_space=pltpu.VMEM),
        scratch_shapes=[
            pltpu.VMEM((vecs, size), f32),
            pltpu.VMEM((2, count), jnp.int32),
            pltpu.VMEM((1, count), jnp.int32),
            pltpu.VMEM((rows * cols, LANES), jnp.int32),
            pltpu.SMEM((rows * cols, LANES), jnp.int32),
            pltpu.VMEM((count, size, size), f32),
            pltpu.VMEM(grid + block, f32),
            pltpu.VMEM((ITERS, cols) + block, f32),
            pltpu.VMEM((ITERS, cols) + block, f32),
            pltpu.VMEM((ITERS, cols) + block, f32),
            pltpu.VMEM(grid + block, f32),
            pltpu.VMEM(grid + block, f32),
            pltpu.VMEM((ITERS, lines) + block, f32),
            pltpu.VMEM((ITERS, lines) + block, f32),
            pltpu.VMEM((cols, 2 * vecs, size), jnp.bfloat16),
            pltpu.VMEM((cols, size, 2 * vecs), f32),
            pltpu.VMEM((rows * cols if kept else 1, 2, size, size), jnp.bfloat16),
            dma,
            dma((4,)),
            dma(grid), dma(grid),
            dma((ITERS, lines, 2)), dma((ITERS, lines, 2)),
            dma((ITERS, cols)), dma((ITERS, cols)),
            dma(grid), dma(grid),
            dma((ITERS, lines, 2)), dma((ITERS, lines, 2)),
            dma((ITERS, lines)), dma((ITERS, lines)),
            dma((ITERS, cols)), dma((ITERS, cols)),
        ],
        compiler_params=pltpu.CompilerParams(
            collective_id=0, has_side_effects=True, vmem_limit_bytes=48 * 1024 * 1024
        ),
    )(vectors.T, tile_coords[0, 0].T, tile_valid[0], stiff_tiles[0, 0]).T


def solution(mesh):
    placed = (
        P(("row", "col"), None),
        P("row", "col", None, None, None),
        P("row", "col", None, None),
        P("row", "col", None),
    )
    return jax.shard_map(
        functools.partial(local, mesh.shape["row"], mesh.shape["col"]),
        mesh=mesh, in_specs=placed, out_specs=P(("row", "col"), None), check_vma=False,
    )
```
